256 devices in a mesh: seq: 16 (over x, y), mp: 16 (over z, core).
Axes of the slice: x: 4, y: 4, z: 8, core: 2. Of those that a mesh axis runs over, the one named last changes fastest.
Arguments:
- hidden: bfloat16 [12288, 4096], P('seq', 'mp'), may hold values from -40 to 40
- encodings: bfloat16 [512, 256, 896], P('seq', 'mp'), may hold values from -32 to 32
- span_owner: int32 [192, 1], replicated, may hold values from 0 to 15; in each aligned block of 12 rows (0 to 11, 12 to 23, ...) at most 2 rows name the same one
- w_query: bfloat16 [4096, 4096], P(None, 'mp'), may hold values from -2 to 2
- w_key: bfloat16 [896, 4096], P(None, 'mp'), may hold values from -2 to 2
- w_value: bfloat16 [896, 4096], P(None, 'mp'), may hold values from -0.1875 to 0.1875
- w_out: bfloat16 [4096, 4096], P('mp'), may hold values from -0.5 to 0.5
- cotangent: bfloat16 [12288, 4096], P('seq', 'mp'), may hold values from -6 to 6
Outputs:
- branch: bfloat16 [12288, 4096], P('seq', 'mp')
- grad_hidden: bfloat16 [12288, 4096], P('seq', 'mp')
- grad_encodings: bfloat16 [512, 256, 896], P('seq', 'mp')
The draws below stay inside these ranges and needn't reach their ends.
Inputs may be any that keep to these rules, and one draw needn't show every extreme that they name: `span_owner`: in each decoder shard's 12 spans (aligned blocks of rows) no encoder shard is named more than 2 times, and in every draw some shard of some block is named exactly 2 times.
All inputs are finite; a program needn't handle non-finite values.
Results may differ from the reference program's by a relative error of at most 0.025.
Values may be sent and summed in bfloat16 or wider, within the bound.
No kernel may reach another device: no remote copies, remote signals or barrier semaphores. Data moves between devices by JAX's collectives and lax.ppermute only.
A program may use at most 128 MiB of HBM per device.

```python
import math
import jax
import jax.numpy as jnp
import numpy as np
from jax import lax

D = 4096
HEADS = 32
DH = 128
DE = 896
SPAN = 64
SPANS_DEV = 12
NR = 256
SPANS = 192
TOKENS = 12288
CAP = 2
SLOTS = 512
N_SEQ = 16
N_MP = 16


def shared_base(key):
    return jnp.clip(jax.random.normal(jax.random.fold_in(key, 202), (DE, HEADS * DH), jnp.float32), -6.0, 6.0)


def draw_hidden(key, part):
    key = jax.random.fold_in(key, 1)
    values_base = jnp.clip(jax.random.normal(key, (TOKENS, D), jnp.float32), -6.0, 6.0)
    return values_base.astype(jnp.bfloat16)


def draw_encodings(key, part):
    key = jax.random.fold_in(key, 2)
    values_base = jnp.clip(jax.random.normal(key, (SLOTS, NR, DE), jnp.float32), -6.0, 6.0)
    return values_base.astype(jnp.bfloat16)


def draw_w_query(key, part):
    key = jax.random.fold_in(key, 3)
    private_part = jnp.clip(jax.random.normal(key, (D, HEADS * DH), jnp.float32), -6.0, 6.0) * D ** (-0.5)
    return private_part.astype(jnp.bfloat16)


def draw_w_key(key, part):
    common = shared_base(key)
    return (common * DE ** (-0.5)).astype(jnp.bfloat16)


def block_levels(key, dims, pieces, least, high):
    level = 1.0
    for axis_at, blocks in pieces:
        steps = jax.random.uniform(jax.random.fold_in(jax.random.fold_in(key, 6), axis_at), (blocks,), jnp.float32, least / len(pieces), high / len(pieces))
        level = level * jnp.repeat(jnp.exp(steps), dims[axis_at] // blocks).reshape((-1,) + (1,) * (len(dims) - 1 - axis_at))
    return level


def assign_block(own_key, own, number, rows, count, top, bound, skew):
    sequence = jax.random.permutation(own_key, count)
    crowded, usual = portions_of(count, rows * top, bound, skew, True), portions_of(count, rows * top, bound, skew, False)
    places = jnp.arange(count)

    def named(sizes, rotation):
        used = int((sizes > 0).sum())
        fixed = max(1, used // 4)
        moved = fixed + (places - fixed + rotation * (used - fixed)) % max(1, count - fixed)
        return jnp.zeros((count,), jnp.int32).at[sequence[jnp.where(places < fixed, places, moved)]].set(jnp.asarray(sizes, jnp.int32))

    sizes = jnp.where(number % 4 == 0, named(crowded, number // 4), named(usual, number - number // 4 - 1))
    mixed = jax.random.permutation(jax.random.fold_in(own, 3), count)
    donor, taker = mixed[0:count // 2 * 2:2], mixed[1:count // 2 * 2:2]
    slack = jnp.minimum(sizes[donor] - 1, bound - sizes[taker]) // 2
    slack = jnp.where((donor == sequence[0]) | (taker == sequence[0]) | (sizes[taker] == 0), 0, jnp.maximum(slack, 0))
    moved = jax.random.randint(jax.random.fold_in(own, 4), (count // 2,), 0, 1 << 20) % (slack + 1)
    sizes = sizes.at[donor].add(-moved).at[taker].add(moved)
    items = jnp.searchsorted(jnp.cumsum(sizes), jnp.arange(rows * top), side="right").astype(jnp.int32)
    grid = items.reshape(top, rows).T
    grid = grid[jax.random.permutation(jax.random.fold_in(own, 1), rows)]
    rotation = jax.random.randint(jax.random.fold_in(own, 2), (rows, 1), 0, top)
    return jnp.take_along_axis(grid, (jnp.arange(top)[None, :] + rotation) % top, axis=1)


def portions_of(amount, total, most, slope, full):
    portions = [(1 << 20) // math.isqrt(rank ** slope) + 1 for rank in range(1, amount + 1)]
    largest = most if full else min(most, max(-(-total // amount), total * portions[0] // sum(portions)))
    least = 1 if total - largest >= amount - 1 else 0
    counts, spare = [largest] + [least] * (amount - 1), total - largest - least * (amount - 1)
    while spare > 0:
        free = [i for i in range(1, amount) if counts[i] < largest] or [i for i in range(1, amount) if counts[i] < most]
        pool, left = sum([portions[i] for i in free]), spare
        for i in free:
            more = min(most - counts[i], max(1, left * portions[i] // pool), spare)
            counts[i] = counts[i] + more
            spare = spare - more
    return np.array(counts)


def normal_values(key, shape, width, limit, pieces=(), kind=jnp.bfloat16):
    loudness = block_levels(key, shape, pieces, -0.22, 0.18) if pieces else 1.0
    values = jax.random.normal(key, shape, jnp.float32) * width * loudness
    return jnp.minimum(jnp.maximum(values, -limit), limit).astype(kind)


def setup_inputs(seed: int = 0) -> dict:
    arg_keys = jax.random.split(jax.random.key(seed), 9)
    hidden = draw_hidden(jax.random.fold_in(arg_keys[8], 71), 0)
    encodings = draw_encodings(jax.random.fold_in(arg_keys[8], 71), 0)
    span_owner_keys = jax.random.split(jax.random.fold_in(arg_keys[2], 1), SPANS // SPANS_DEV)
    span_owner_turns = jax.random.permutation(jax.random.fold_in(arg_keys[2], 3), SPANS // SPANS_DEV)
    span_owner = jax.vmap(lambda own, number: assign_block(jax.random.fold_in(arg_keys[2], 2), own, number, SPANS_DEV, N_SEQ, 1, CAP, 2))(span_owner_keys, span_owner_turns).reshape((SPANS, 1))
    w_query = draw_w_query(jax.random.fold_in(arg_keys[8], 71), 0)
    w_key = draw_w_key(jax.random.fold_in(arg_keys[8], 71), 0)
    w_value = normal_values(arg_keys[5], (DE, HEADS * DH), DE ** -0.5, 0.1875, ((1, 16),))
    w_out = normal_values(arg_keys[6], (HEADS * DH, D), DH ** -0.5, 0.5, ((0, 16),))
    cotangent = normal_values(arg_keys[7], (TOKENS, D), 1.0, 6.0, ((0, 16), (1, 16)))
    return {"hidden": hidden, "encodings": encodings, "span_owner": span_owner, "w_query": w_query, "w_key": w_key, "w_value": w_value, "w_out": w_out, "cotangent": cotangent}


def span_slots(owners):
    positions = jnp.arange(SPANS, dtype=jnp.int32)
    shard_of = (positions // SPANS_DEV).astype(jnp.int32)
    earlier = (owners[:, None] == owners[None, :]) & (shard_of[:, None] == shard_of[None, :]) & (positions[None, :] < positions[:, None])
    rank_in_owner = jnp.sum(earlier.astype(jnp.int32), axis=1).astype(jnp.int32)
    return (owners * (N_SEQ * CAP) + shard_of * CAP + rank_in_owner).astype(jnp.int32)


def attend(query_sets, key_sets, value_sets):
    scores = jnp.einsum("sqhe,srhe->shqr", query_sets.astype(jnp.float32), key_sets.astype(jnp.float32)) * (DH ** -0.5)
    highest = jnp.max(scores, axis=-1, keepdims=True)
    raised = jnp.exp(scores - highest)
    weights = raised / jnp.sum(raised, axis=-1, keepdims=True)
    weights_low = weights.astype(jnp.bfloat16)
    attended = jnp.einsum("shqr,srhe->sqhe", weights_low.astype(jnp.float32), value_sets.astype(jnp.float32)).astype(jnp.bfloat16)
    return weights, weights_low, attended


def attend_back(query_sets, key_sets, value_sets, weights, weights_low, grad_sets):
    grad_weights = jnp.einsum("sqhe,srhe->shqr", grad_sets.astype(jnp.float32), value_sets.astype(jnp.float32))
    inner_sum = jnp.sum(weights * grad_weights, axis=-1, keepdims=True)
    grad_scores = (weights * (grad_weights - inner_sum) * (DH ** -0.5)).astype(jnp.bfloat16).astype(jnp.float32)
    grad_queries = jnp.einsum("shqr,srhe->sqhe", grad_scores, key_sets.astype(jnp.float32))
    grad_keys = jnp.einsum("shqr,sqhe->srhe", grad_scores, query_sets.astype(jnp.float32))
    grad_values = jnp.einsum("shqr,sqhe->srhe", weights_low.astype(jnp.float32), grad_sets.astype(jnp.float32))
    return grad_queries, grad_keys, grad_values


def reference(hidden, encodings, span_owner, w_query, w_key, w_value, w_out, cotangent):
    slot_rows = span_slots(span_owner[:, 0].astype(jnp.int32))
    span_enc = jnp.take(encodings, slot_rows, axis=0).reshape(SPANS * NR, DE)
    columns = HEADS * DH // N_MP
    groups = columns // DH
    pad_front = jnp.zeros((1, columns), jnp.bfloat16)
    pad_back = jnp.zeros((SPAN - 1, columns), jnp.bfloat16)
    zero_span = jnp.zeros((1, NR, groups, DH), jnp.bfloat16)

    def one_group(partials, group_index):
        branch_sum, hidden_sum, enc_sum = partials
        first_col = group_index * columns
        query_cols = lax.dynamic_slice_in_dim(w_query, first_col, columns, 1)
        key_cols = lax.dynamic_slice_in_dim(w_key, first_col, columns, 1)
        value_cols = lax.dynamic_slice_in_dim(w_value, first_col, columns, 1)
        out_rows = lax.dynamic_slice_in_dim(w_out, first_col, columns, 0)
        queries = jnp.dot(hidden, query_cols, preferred_element_type=jnp.float32).astype(jnp.bfloat16)
        keys = jnp.dot(span_enc, key_cols, preferred_element_type=jnp.float32).astype(jnp.bfloat16).reshape(SPANS, NR, groups, DH)
        values = jnp.dot(span_enc, value_cols, preferred_element_type=jnp.float32).astype(jnp.bfloat16).reshape(SPANS, NR, groups, DH)
        key_sets = jnp.concatenate([zero_span, keys], axis=0)
        value_sets = jnp.concatenate([zero_span, values], axis=0)
        query_sets = jnp.concatenate([pad_front, queries, pad_back], axis=0).reshape(SPANS + 1, SPAN, groups, DH)
        weights, weights_low, attended_sets = attend(query_sets, key_sets, value_sets)
        attended = attended_sets.reshape(-1, columns)[1:TOKENS + 1]
        branch_part = lax.optimization_barrier(jnp.dot(attended, out_rows, preferred_element_type=jnp.float32).astype(jnp.bfloat16))
        grad_attended = jnp.dot(cotangent, out_rows.T, preferred_element_type=jnp.float32).astype(jnp.bfloat16)
        grad_sets = jnp.concatenate([pad_front, grad_attended, pad_back], axis=0).reshape(SPANS + 1, SPAN, groups, DH)
        grad_q_sets, grad_k_sets, grad_v_sets = attend_back(query_sets, key_sets, value_sets, weights, weights_low, grad_sets)
        grad_queries = grad_q_sets.reshape(-1, columns)[1:TOKENS + 1].astype(jnp.bfloat16)
        hidden_part = lax.optimization_barrier(jnp.dot(grad_queries, query_cols.T, preferred_element_type=jnp.float32).astype(jnp.bfloat16))
        grad_keys = grad_k_sets[1:].reshape(SPANS * NR, columns).astype(jnp.bfloat16)
        grad_values = grad_v_sets[1:].reshape(SPANS * NR, columns).astype(jnp.bfloat16)
        enc_part = jnp.dot(grad_keys, key_cols.T, preferred_element_type=jnp.float32) + jnp.dot(grad_values, value_cols.T, preferred_element_type=jnp.float32)
        enc_part = lax.optimization_barrier(enc_part.astype(jnp.bfloat16))
        return (branch_sum + branch_part.astype(jnp.float32), hidden_sum + hidden_part.astype(jnp.float32), enc_sum + enc_part.astype(jnp.float32)), None

    start_sums = (jnp.zeros((TOKENS, D), jnp.float32), jnp.zeros((TOKENS, D), jnp.float32), jnp.zeros((SPANS * NR, DE), jnp.float32))
    sums, unused = lax.scan(one_group, start_sums, jnp.arange(N_MP, dtype=jnp.int32))
    branch = sums[0].astype(jnp.bfloat16)
    grad_hidden = sums[1].astype(jnp.bfloat16)
    grad_spans = sums[2].astype(jnp.bfloat16).reshape(SPANS, NR, DE)
    grad_encodings = jnp.zeros((SLOTS, NR, DE), jnp.bfloat16).at[slot_rows].set(grad_spans)
    return branch, grad_hidden, grad_encodings
```

```python
import jax
import jax.numpy as jnp
from jax import lax
from jax.experimental import pallas as pl
from jax.experimental.pallas import tpu as pltpu
from jax.sharding import PartitionSpec as P

DH = 128
SPAN = 64
LEAD = SPAN - 1
CORES = 2
F32 = jnp.float32
BF16 = jnp.bfloat16
NT = (((1,), (1,)), ((), ()))
TN = (((0,), (0,)), ((), ()))


def ring_pairs(count):
    chips = count // CORES
    up = [(CORES * i, CORES * ((i + 1) % chips)) for i in range(chips)]
    down = [(CORES * i + 1, CORES * ((i - 1) % chips) + 1) for i in range(chips)]
    return up + down


def swap_cores(value):
    count = lax.axis_size("mp")
    return lax.ppermute(value, "mp", [(i, i ^ 1) for i in range(count)])


def from_behind(value, axis, steps):
    count = lax.axis_size(axis)
    initial, last = (max(0, -steps), min(count, count - steps))
    return lax.ppermute(value, axis, [(source, source + steps) for source in range(initial, last)])


def ring_gather(block, pairs, chips):
    blocks = [block]
    for _ in range(chips - 1):
        blocks.append(lax.ppermute(blocks[-1], "mp", pairs))
    return blocks


def ring_reduce(term, pairs, chips):
    total = term(1)
    for place in range(2, chips + 1):
        received = lax.ppermute(total.astype(BF16), "mp", pairs)
        total = term(place % chips) + received.astype(F32)
    return total.astype(BF16)


def attention_kernel(q1, q2, g1, g2, kv_own, kv_sib, att_ref, gq_ref, gkv_own, gkv_sib):
    chips, spans, rows, width = kv_own.shape
    columns = width // 2
    scale = DH ** (-0.5)
    for u in range(spans):
        tok = slice(u * SPAN, (u + 1) * SPAN)
        queries = (q1[tok, :] + q2[tok, :].astype(F32)).astype(BF16)
        grads = (g1[tok, :] + g2[tok, :].astype(F32)).astype(BF16)
        key_values = jnp.concatenate(
            [
                kv_own[:, u, :, :].reshape(chips * rows, width),
                kv_sib[:, u, :, :].reshape(chips * rows, width),
            ],
            axis=0,
        )
        half = chips * rows
        for h in range(columns // DH):
            col = slice(h * DH, (h + 1) * DH)
            vcol = slice(columns + h * DH, columns + (h + 1) * DH)
            q, g = queries[:, col], grads[:, col]
            k, v = key_values[:, col], key_values[:, vcol]
            scores = lax.dot_general(q, k, NT, preferred_element_type=F32) * scale
            grad_w = lax.dot_general(g, v, NT, preferred_element_type=F32)
            raised = jnp.exp(scores - jnp.max(scores, axis=-1, keepdims=True))
            weights = raised / jnp.sum(raised, axis=-1, keepdims=True)
            low = weights.astype(BF16)
            inner = jnp.sum(weights * grad_w, axis=-1, keepdims=True)
            grad_s = (weights * (grad_w - inner) * scale).astype(BF16)
            att_ref[tok, col] = jnp.dot(low, v, preferred_element_type=F32).astype(BF16)
            gq_ref[tok, col] = jnp.dot(grad_s, k, preferred_element_type=F32).astype(BF16)
            gk = lax.dot_general(grad_s, q, TN, preferred_element_type=F32).astype(BF16)
            gv = lax.dot_general(low, g, TN, preferred_element_type=F32).astype(BF16)
            gkv_own[:, u, :, col] = gk[:half].reshape(chips, rows, DH)
            gkv_sib[:, u, :, col] = gk[half:].reshape(chips, rows, DH)
            gkv_own[:, u, :, vcol] = gv[:half].reshape(chips, rows, DH)
            gkv_sib[:, u, :, vcol] = gv[half:].reshape(chips, rows, DH)


def attention(q1, q2, g1, g2, kv_own, kv_sib, per_step=4):
    chips, spans, rows, width = kv_own.shape
    tokens, columns = q1.shape
    tok = pl.BlockSpec((per_step * SPAN, columns), lambda i: (i, 0))
    kvs = pl.BlockSpec((chips, per_step, rows, width), lambda i: (0, i, 0, 0))
    low = jax.ShapeDtypeStruct((tokens, columns), BF16)
    kv_type = jax.ShapeDtypeStruct(kv_own.shape, BF16)
    return pl.pallas_call(
        attention_kernel,
        grid=(spans // per_step,),
        in_specs=[tok, tok, tok, tok, kvs, kvs],
        out_specs=[tok, tok, kvs, kvs],
        out_shape=[low, low, kv_type, kv_type],
        compiler_params=pltpu.CompilerParams(vmem_limit_bytes=48 * 1024 * 1024),
    )(q1, q2, g1, g2, kv_own, kv_sib)


def on_device(hidden, encodings, span_owner, w_query, w_key, w_value, w_out, cotangent):
    seq_count = lax.axis_size("seq")
    shard_index = lax.axis_index("seq")
    mp_count = lax.axis_size("mp")
    chips = mp_count // CORES
    place = lax.axis_index("mp")
    core = place % CORES
    chip = place // CORES
    pairs = ring_pairs(mp_count)
    heading = 1 - 2 * core
    origin = [(chip - heading * k + chips) % chips for k in range(chips)]

    capacity = encodings.shape[0] // seq_count
    token_count, width = hidden.shape
    span_count = token_count // SPAN
    rows, depth = encodings.shape[1:]
    columns = w_query.shape[1]

    owners = lax.dynamic_slice_in_dim(span_owner[:, 0], shard_index * span_count, span_count)
    positions = jnp.arange(span_count, dtype=jnp.int32)
    earlier = (owners[:, None] == owners[None, :]) & (positions[None, :] < positions[:, None])
    picked = owners * capacity + jnp.sum(earlier.astype(jnp.int32), axis=1)

    def shifted(value):
        after = from_behind(value[:SPAN], "seq", -1)
        return jnp.concatenate([value[LEAD:], after[:LEAD]], axis=0)

    def unshifted(value):
        before = from_behind(value[token_count - SPAN:], "seq", 1)
        return jnp.concatenate([before[1:], value[: token_count - LEAD]], axis=0)

    wq_parts = w_query.reshape(chips, CORES, width, columns)
    wq_mine = lax.dynamic_index_in_dim(wq_parts, core, 1, keepdims=False)
    wq_other = lax.dynamic_index_in_dim(wq_parts, 1 - core, 1, keepdims=False)
    wq_full = jnp.concatenate([wq_mine, swap_cores(wq_other)], axis=2)
    wo_parts = w_out.reshape(columns, chips, CORES, width)
    wo_mine = lax.dynamic_index_in_dim(wo_parts, core, 2, keepdims=False)
    wo_other = lax.dynamic_index_in_dim(wo_parts, 1 - core, 2, keepdims=False)
    wo_full = jnp.concatenate([wo_mine, swap_cores(wo_other)], axis=0)
    wkv_mine = jnp.concatenate([w_key, w_value], axis=1)
    wkv_full = jnp.concatenate([wkv_mine, swap_cores(wkv_mine)], axis=1)

    wq_at = [lax.dynamic_index_in_dim(wq_full, origin[k], 0, keepdims=False) for k in range(chips)]
    wo_at = [lax.dynamic_index_in_dim(wo_full, origin[k], 1, keepdims=False) for k in range(chips)]

    received = lax.all_to_all(encodings, "seq", split_axis=0, concat_axis=0, tiled=True)
    shard_part = jnp.take(received, picked, axis=0).reshape(span_count * rows, depth)

    hidden_blocks = ring_gather(shifted(hidden), pairs, chips)
    cot_blocks = ring_gather(shifted(cotangent), pairs, chips)
    enc_blocks = ring_gather(shard_part, pairs, chips)

    queries = sum(
        jnp.dot(block, weight, preferred_element_type=F32)
        for block, weight in zip(hidden_blocks, wq_at)
    )
    grads = sum(
        lax.dot_general(block, weight, NT, preferred_element_type=F32)
        for block, weight in zip(cot_blocks, wo_at)
    )
    q_other = swap_cores(queries[:, columns:].astype(BF16))
    g_other = swap_cores(grads[:, columns:].astype(BF16))
    key_values = [
        jnp.dot(block, wkv_full, preferred_element_type=F32).astype(BF16) for block in enc_blocks
    ]
    kv_own = jnp.stack([kv[:, : 2 * columns] for kv in key_values])
    kv_send = jnp.stack([kv[:, 2 * columns:] for kv in key_values])
    kv_sib = swap_cores(kv_send)
    kv_shape = (chips, span_count, rows, 2 * columns)
    attended, grad_queries, gkv_own, gkv_sib = attention(
        queries[:, :columns],
        q_other,
        grads[:, :columns],
        g_other,
        kv_own.reshape(kv_shape),
        kv_sib.reshape(kv_shape),
    )
    gkv_full = jnp.concatenate([gkv_own, swap_cores(gkv_sib)], axis=3).reshape(
        chips, span_count * rows, 4 * columns
    )
    att_full = jnp.concatenate([attended, swap_cores(attended)], axis=1)
    gq_full = jnp.concatenate([grad_queries, swap_cores(grad_queries)], axis=1)

    enc_share = ring_reduce(
        lambda k: lax.dot_general(gkv_full[k], wkv_full, NT, preferred_element_type=F32),
        pairs,
        chips,
    )
    branch = ring_reduce(
        lambda k: jnp.dot(att_full, wo_at[k], preferred_element_type=F32), pairs, chips
    )
    grad_hidden = ring_reduce(
        lambda k: lax.dot_general(gq_full, wq_at[k], NT, preferred_element_type=F32),
        pairs,
        chips,
    )
    outgoing = (
        jnp.zeros(encodings.shape, BF16)
        .at[picked]
        .set(enc_share.reshape(span_count, rows, depth))
    )
    grad_encodings = lax.all_to_all(outgoing, "seq", split_axis=0, concat_axis=0, tiled=True)
    return (unshifted(branch), unshifted(grad_hidden), grad_encodings)


def solution(mesh):
    return jax.shard_map(
        on_device,
        mesh=mesh,
        in_specs=(
            P("seq", "mp"),
            P("seq", "mp", None),
            P(),
            P(None, "mp"),
            P(None, "mp"),
            P(None, "mp"),
            P("mp", None),
            P("seq", "mp"),
        ),
        out_specs=(P("seq", "mp"), P("seq", "mp"), P("seq", "mp", None)),
        check_vma=False,
    )
```

```python
import functools

import jax
import jax.numpy as jnp
from jax import lax
from jax.experimental import pallas as pl
from jax.experimental.pallas import tpu as pltpu
from jax.sharding import PartitionSpec as P

DH = 128
SPAN = 64
LEAD = SPAN - 1
CORES = 2
F32 = jnp.float32
BF16 = jnp.bfloat16
NT = (((1,), (1,)), ((), ()))
NN = (((1,), (0,)), ((), ()))
TN = (((0,), (0,)), ((), ()))


def ring_pairs(count):
    chips = count // CORES
    up = [(CORES * i, CORES * ((i + 1) % chips)) for i in range(chips)]
    down = [(CORES * i + 1, CORES * ((i - 1) % chips) + 1) for i in range(chips)]
    return up + down


def swap_cores(value):
    count = lax.axis_size("mp")
    return lax.ppermute(value, "mp", [(i, i ^ 1) for i in range(count)])


def ring_steps(block, pairs, steps):
    blocks = []
    for _ in range(steps):
        block = lax.ppermute(block, "mp", pairs)
        blocks.append(block)
    return blocks


def ring_reduce(term, pairs, places, total=None):
    for place in places:
        own = term(place)
        if total is not None:
            own = own + lax.ppermute(total, "mp", pairs).astype(F32)
        total = own.astype(BF16)
    return total


def one_way(count, step):
    return [(i, (i + CORES * step) % count) for i in range(count)]


def both_ways_gather(block, up, down, chips):
    steps = chips // 2 - 1
    half = block.shape[0] // 2
    behind, ahead = ring_steps(block, up, steps), ring_steps(block, down, steps)
    opposite = jnp.concatenate(
        [
            lax.ppermute(behind[-1][:half], "mp", up),
            lax.ppermute(ahead[-1][half:], "mp", down),
        ],
        axis=0,
    )
    return [block, *behind, *ahead, opposite]


def both_ways_reduce(term, opposite, up, down, chips):
    steps = chips // 2 - 1
    half = opposite[0].shape[0]
    got_up = lax.ppermute(opposite[0], "mp", up).astype(F32)
    got_down = lax.ppermute(opposite[1], "mp", down).astype(F32)
    to_up, to_down = term(chips - 2), term(steps)
    to_up = jnp.concatenate([to_up[:half] + got_up, to_up[half:]], axis=0)
    to_down = jnp.concatenate([to_down[:half], to_down[half:] + got_down], axis=0)
    for left in range(steps - 1, -1, -1):
        got_up = lax.ppermute(to_up.astype(BF16), "mp", up).astype(F32)
        got_down = lax.ppermute(to_down.astype(BF16), "mp", down).astype(F32)
        if left:
            to_up, to_down = term(steps + left) + got_up, term(left) + got_down
    return (term(0) + got_up + got_down).astype(BF16)


def after(value, *earlier):
    return lax.optimization_barrier((value, *earlier))[0]


def ring_weights_kernel(places, wq_own, wq_sib, wo_own, wo_sib, wq_ring, wo_ring):
    columns = wq_own.shape[1]
    wq_ring[0, :, :columns] = wq_own[...]
    wq_ring[0, :, columns:] = wq_sib[...]
    wo_ring[0, :columns, :] = wo_own[...]
    wo_ring[0, columns:, :] = wo_sib[...]


def ring_weights(places, w_query, wq_sib, w_out, wo_sib, width):
    count = places.shape[0]
    columns = w_query.shape[1]
    by_rows = pl.BlockSpec((width, columns), lambda k, at: (at[k], 0))
    by_columns = pl.BlockSpec((columns, width), lambda k, at: (0, at[k]))
    return pl.pallas_call(
        ring_weights_kernel,
        grid_spec=pltpu.PrefetchScalarGridSpec(
            num_scalar_prefetch=1,
            grid=(count,),
            in_specs=[by_rows, by_rows, by_columns, by_columns],
            out_specs=[
                pl.BlockSpec((1, width, CORES * columns), lambda k, at: (k, 0, 0)),
                pl.BlockSpec((1, CORES * columns, width), lambda k, at: (k, 0, 0)),
            ],
        ),
        out_shape=[
            jax.ShapeDtypeStruct((count, width, CORES * columns), BF16),
            jax.ShapeDtypeStruct((count, CORES * columns, width), BF16),
        ],
    )(places, w_query, wq_sib, w_out, wo_sib)


def pick_kernel(picked, held, out):
    for u in range(out.shape[0]):
        out[u] = held[picked[u]]


def pick(held, picked):
    count = picked.shape[0]
    return pl.pallas_call(
        pick_kernel,
        grid_spec=pltpu.PrefetchScalarGridSpec(
            num_scalar_prefetch=1,
            grid=(1,),
            in_specs=[pl.BlockSpec(held.shape, lambda i, at: (0, 0, 0))],
            out_specs=pl.BlockSpec((count, *held.shape[1:]), lambda i, at: (0, 0, 0)),
        ),
        out_shape=jax.ShapeDtypeStruct((count, *held.shape[1:]), BF16),
    )(picked, held)


def place_kernel(picked, shares, out):
    out[...] = jnp.zeros_like(out)
    for u in range(shares.shape[0]):
        out[picked[u]] = shares[u]


def place_shares(shares, picked, slots):
    shape = (slots, *shares.shape[1:])
    return pl.pallas_call(
        place_kernel,
        grid_spec=pltpu.PrefetchScalarGridSpec(
            num_scalar_prefetch=1,
            grid=(1,),
            in_specs=[pl.BlockSpec(shares.shape, lambda i, at: (0, 0, 0))],
            out_specs=pl.BlockSpec(shape, lambda i, at: (0, 0, 0)),
        ),
        out_shape=jax.ShapeDtypeStruct(shape, BF16),
    )(picked, shares)


def project_part_kernel(dims, *refs):
    *blocks, weights, out = refs
    total = None
    for k, block in enumerate(blocks):
        part = lax.dot_general(block[...], weights[k], dims, preferred_element_type=F32)
        total = part if total is None else total + part
    out[...] = total


def project_part(blocks, weights, dims, tile=256):
    tokens, width = blocks[0].shape
    count, wide = len(blocks), CORES * width
    return pl.pallas_call(
        functools.partial(project_part_kernel, dims),
        grid=(tokens // tile,),
        in_specs=[pl.BlockSpec((tile, width), lambda i: (i, 0))] * count
        + [pl.BlockSpec((count, *weights.shape[1:]), lambda i: (0, 0, 0))],
        out_specs=pl.BlockSpec((tile, wide), lambda i: (i, 0)),
        out_shape=jax.ShapeDtypeStruct((tokens, wide), F32),
        compiler_params=pltpu.CompilerParams(vmem_limit_bytes=32 * 1024 * 1024),
    )(*blocks, weights)


def project_rest_kernel(count, *refs):
    hidden, cot = refs[:count], refs[count : 2 * count]
    wq, wo, q_part, g_part, own, sib = refs[2 * count :]
    columns = own.shape[1] // 2
    for at, (blocks, weights, part, dims) in enumerate(
        ((hidden, wq, q_part, NN), (cot, wo, g_part, NT))
    ):
        total = part[...]
        for k, block in enumerate(blocks):
            total += lax.dot_general(block[...], weights[k], dims, preferred_element_type=F32)
        col = slice(at * columns, (at + 1) * columns)
        own[:, col] = total[:, :columns]
        sib[:, col] = total[:, columns:].astype(BF16)


def project_rest(hidden, cot, wq, wo, q_part, g_part, tokens, tile):
    width = hidden[0].shape[1]
    count, wide = len(hidden), CORES * width
    rows = pl.BlockSpec((tile, width), lambda i: (i, 0))
    wide_rows = pl.BlockSpec((tile, wide), lambda i: (i, 0))
    last = wq.shape[0] // count - 1
    return pl.pallas_call(
        functools.partial(project_rest_kernel, count),
        grid=(tokens // tile,),
        in_specs=[rows] * (2 * count)
        + [
            pl.BlockSpec((count, *wq.shape[1:]), lambda i: (last, 0, 0)),
            pl.BlockSpec((count, *wo.shape[1:]), lambda i: (last, 0, 0)),
            wide_rows,
            wide_rows,
        ],
        out_specs=[wide_rows, wide_rows],
        out_shape=[
            jax.ShapeDtypeStruct((tokens, wide), F32),
            jax.ShapeDtypeStruct((tokens, wide), BF16),
        ],
        compiler_params=pltpu.CompilerParams(vmem_limit_bytes=48 * 1024 * 1024),
    )(*hidden, *cot, wq, wo, q_part, g_part)


def key_values_kernel(*refs):
    *blocks, weights, own, sib = refs
    width = own.shape[2]
    for k, block in enumerate(blocks):
        total = jnp.dot(block[...], weights[...], preferred_element_type=F32).astype(BF16)
        own[k] = total[:, :width]
        sib[k] = total[:, width:]


def key_values(blocks, weights):
    rows, depth = blocks[0].shape
    count, width = len(blocks), weights.shape[1] // CORES
    out = jax.ShapeDtypeStruct((count, rows, width), BF16)
    return pl.pallas_call(
        key_values_kernel,
        out_shape=[out, out],
        compiler_params=pltpu.CompilerParams(vmem_limit_bytes=32 * 1024 * 1024),
    )(*blocks, weights)


def attention_kernel(part_count, own, got, own_next, got_next, before, *refs):
    kv_parts, refs = refs[:part_count], refs[part_count:]
    out, out_after, gkv_own, gkv_sib, carry = refs[-5:]
    chips, spans, rows, width = gkv_own.shape
    columns = width // 2
    heads = columns // DH
    half = chips * rows
    scale = DH ** (-0.5)
    tokens = own.shape[0]

    here = own[...] + got[...].astype(F32)
    following = own_next[...] + got_next[...].astype(F32)
    asked = jnp.concatenate([here[LEAD:], following[:LEAD]], axis=0).astype(BF16)

    todo = []
    for u in range(spans):
        tok = slice(u * SPAN, (u + 1) * SPAN)
        key_values = jnp.concatenate(
            [part[:, u, :, :].reshape(part.shape[0] * rows, width) for part in kv_parts],
            axis=0,
        )
        for h in range(heads):
            col = slice(h * DH, (h + 1) * DH)
            vcol = slice(columns + h * DH, columns + (h + 1) * DH)
            todo.append((u, col, vcol, asked[tok, col], asked[tok, vcol], key_values[:, col], key_values[:, vcol]))
    scores = [lax.dot_general(q, k, NT, preferred_element_type=F32) * scale for _, _, _, q, _, k, _ in todo]
    grad_w = [lax.dot_general(g, v, NT, preferred_element_type=F32) for _, _, _, _, g, _, v in todo]
    raised = [jnp.exp(x - jnp.max(x, axis=-1, keepdims=True)) for x in scores]
    weights = [x * (1.0 / jnp.sum(x, axis=-1, keepdims=True)) for x in raised]
    low = [x.astype(BF16) for x in weights]
    inner = [jnp.sum(x * y, axis=-1, keepdims=True) for x, y in zip(weights, grad_w)]
    grad_s = [(x * (y - z) * scale).astype(BF16) for x, y, z in zip(weights, grad_w, inner)]
    attended = [jnp.dot(x, t[6], preferred_element_type=F32) for x, t in zip(low, todo)]
    grad_q = [jnp.dot(x, t[5], preferred_element_type=F32) for x, t in zip(grad_s, todo)]
    for (u, col, vcol, q, g, _, _), x, y in zip(todo, low, grad_s):
        gk = lax.dot_general(y, q, TN, preferred_element_type=F32).astype(BF16)
        gv = lax.dot_general(x, g, TN, preferred_element_type=F32).astype(BF16)
        gkv_own[:, u, :, col] = gk[:half].reshape(chips, rows, DH)
        gkv_sib[:, u, :, col] = gk[half:].reshape(chips, rows, DH)
        gkv_own[:, u, :, vcol] = gv[:half].reshape(chips, rows, DH)
        gkv_sib[:, u, :, vcol] = gv[half:].reshape(chips, rows, DH)
    by_span = [
        jnp.concatenate(attended[u * heads : (u + 1) * heads] + grad_q[u * heads : (u + 1) * heads], axis=1)
        for u in range(spans)
    ]
    answers = jnp.concatenate(by_span, axis=0)
    earlier = jnp.where(pl.program_id(0) == 0, before[...].astype(F32), carry[...])
    out[...] = jnp.concatenate([earlier[:LEAD], answers[: tokens - LEAD]], axis=0).astype(BF16)
    left = jnp.concatenate([answers[tokens - LEAD:], jnp.zeros((1, answers.shape[1]), F32)], axis=0)
    carry[...] = left
    out_after[...] = left.astype(BF16)


def attention(own, got, own_next, got_next, before, kv_parts, first, steps, results=(), per_step=4):
    _, spans, rows, width = kv_parts[0].shape
    chips = sum(part.shape[0] for part in kv_parts) // CORES
    tokens, wide = own.shape
    following = first + 1 if own_next is own else 0
    tok = pl.BlockSpec((per_step * SPAN, wide), lambda i: (first + i, 0))
    nexts = pl.BlockSpec((SPAN, wide), lambda i: ((following + i) * per_step, 0))
    whole = pl.BlockSpec((SPAN, wide), lambda i: (0, 0))

    def kvs(count):
        return pl.BlockSpec((count, per_step, rows, width), lambda i: (0, first + i, 0, 0))

    kv_type = jax.ShapeDtypeStruct((chips, spans, rows, width), BF16)
    given = 5 + len(kv_parts)
    return pl.pallas_call(
        functools.partial(attention_kernel, len(kv_parts)),
        grid=(steps,),
        in_specs=[tok, tok, nexts, nexts, whole]
        + [kvs(part.shape[0]) for part in kv_parts]
        + [pl.BlockSpec(memory_space=pl.ANY)] * len(results),
        out_specs=[tok, whole, kvs(chips), kvs(chips)],
        out_shape=[
            jax.ShapeDtypeStruct((tokens, wide), BF16),
            jax.ShapeDtypeStruct((SPAN, wide), BF16),
            kv_type,
            kv_type,
        ],
        scratch_shapes=[pltpu.VMEM((SPAN, wide), F32)],
        input_output_aliases=dict(zip(range(given, given + len(results)), (0, 2, 3))),
        compiler_params=pltpu.CompilerParams(vmem_limit_bytes=48 * 1024 * 1024),
    )(own, got, own_next, got_next, before, *kv_parts, *results)


def on_device(hidden, encodings, span_owner, w_query, w_key, w_value, w_out, cotangent):
    seq_count = lax.axis_size("seq")
    shard_index = lax.axis_index("seq")
    mp_count = lax.axis_size("mp")
    chips = mp_count // CORES
    place = lax.axis_index("mp")
    core = place % CORES
    chip = place // CORES
    pairs = ring_pairs(mp_count)
    heading = 1 - 2 * core
    origin = [(chip - heading * k + chips) % chips for k in range(chips)]

    capacity = encodings.shape[0] // seq_count
    token_count, width = hidden.shape
    span_count = token_count // SPAN
    rows, depth = encodings.shape[1:]
    columns = w_query.shape[1]

    owners = lax.dynamic_slice_in_dim(span_owner[:, 0], shard_index * span_count, span_count)
    positions = jnp.arange(span_count, dtype=jnp.int32)
    earlier = (owners[:, None] == owners[None, :]) & (positions[None, :] < positions[:, None])
    picked = owners * capacity + jnp.sum(earlier.astype(jnp.int32), axis=1)

    def to_shard(value, steps, across):
        shards = range(max(0, -steps), min(seq_count, seq_count - steps))
        moves = [
            (d * mp_count + i, (d + steps) * mp_count + (i ^ across))
            for d in shards
            for i in range(mp_count)
        ]
        return lax.ppermute(value, ("seq", "mp"), moves)

    up, down = one_way(mp_count, 1), one_way(mp_count, -1)

    wk_sib, wv_sib = swap_cores(w_key), swap_cores(w_value)
    wkv_full = jnp.concatenate([w_key, w_value, wk_sib, wv_sib], axis=1)
    places = jnp.stack([CORES * source + core for source in origin])
    wq_ring, wo_ring = ring_weights(
        places, w_query, swap_cores(w_query), w_out, swap_cores(w_out), width
    )

    received = lax.all_to_all(
        after(encodings, wk_sib), "seq", split_axis=0, concat_axis=0, tiled=True
    )
    shard_part = pick(received, picked).reshape(span_count * rows, depth)
    early = chips // 2
    hidden_blocks = [hidden] + ring_steps(hidden, pairs, early)
    cot_blocks = [cotangent] + ring_steps(cotangent, pairs, early)
    hidden_last, cot_last, wq_ring, wo_ring = lax.optimization_barrier(
        (hidden_blocks.pop(), cot_blocks.pop(), wq_ring, wo_ring)
    )
    hidden_late = [hidden_last] + ring_steps(hidden_last, pairs, chips - early - 2)
    cot_late = [cot_last] + ring_steps(cot_last, pairs, chips - early - 2)
    enc_blocks = both_ways_gather(shard_part, up, down, chips)

    q_part = project_part(hidden_blocks, wq_ring, NN)
    g_part = project_part(cot_blocks, wo_ring, NT)
    kv_own_a, kv_send_a = key_values([enc_blocks[k] for k in (0, 1, 2, 4, 5)], wkv_full)
    hidden_last, cot_last, q_part, g_part, kv_own_a, kv_send_a = lax.optimization_barrier(
        (hidden_late[-1], cot_late[-1], q_part, g_part, kv_own_a, kv_send_a)
    )
    hidden_late[-1], cot_late[-1] = hidden_last, cot_last
    hidden_late += ring_steps(hidden_last, pairs, 1)
    cot_late += ring_steps(cot_last, pairs, 1)
    kv_sib_a = swap_cores(kv_send_a)
    kv_own_b, kv_send_b = key_values([enc_blocks[3], enc_blocks[6], enc_blocks[7]], wkv_full)
    kv_sib_b = swap_cores(kv_send_b)
    q_part, g_part, _ = lax.optimization_barrier((q_part, g_part, kv_send_b))
    own, send = project_rest(
        hidden_late, cot_late, wq_ring, wo_ring, q_part, g_part, token_count, 256
    )
    got = swap_cores(send)
    own_after, got_after = to_shard(own[:SPAN], -1, 0), to_shard(send[:SPAN], -1, 1)
    order = [0, 1, 2, 4, 5, 3, 6, 7]
    kv_parts = [
        part.reshape(-1, span_count, rows, 2 * columns)
        for part in (kv_own_a, kv_own_b, kv_sib_a, kv_sib_b)
    ]
    steps = span_count // 4
    nothing = jnp.zeros((SPAN, 2 * columns), BF16)
    answers, answers_after, gkv_own, gkv_sib = attention(
        own, got, own, got, nothing, kv_parts, 0, steps - 1
    )
    answers, answers_after, gkv_own, gkv_sib = attention(
        own,
        got,
        own_after,
        got_after,
        answers_after,
        kv_parts,
        steps - 1,
        1,
        (answers, gkv_own, gkv_sib),
    )
    gkv_full = jnp.concatenate([gkv_own, swap_cores(gkv_sib)], axis=3).reshape(
        chips, span_count * rows, 4 * columns
    )
    answers_got = swap_cores(answers)
    lead_own, lead_got = to_shard(answers_after, 1, 0), to_shard(answers_after, 1, 1)
    answers = answers.at[:SPAN].add(lead_own)
    answers_got = answers_got.at[:SPAN].add(lead_got)
    att_full = jnp.concatenate([answers[:, :columns], answers_got[:, :columns]], axis=1)
    gq_full = jnp.concatenate([answers[:, columns:], answers_got[:, columns:]], axis=1)

    def enc_term(k):
        return lax.dot_general(
            gkv_full[order.index(k)], wkv_full, NT, preferred_element_type=F32
        )

    def branch_term(k):
        return jnp.dot(att_full, wo_ring[k], preferred_element_type=F32)

    def hidden_term(k):
        return lax.dot_general(gq_full, wq_ring[k], NT, preferred_element_type=F32)

    opposite = enc_term(chips - 1).astype(BF16)
    half = opposite.shape[0] // 2
    opposite = (opposite[:half], opposite[half:])
    att_full, gq_full, opposite = lax.optimization_barrier((att_full, gq_full, opposite))
    enc_share = both_ways_reduce(enc_term, opposite, up, down, chips)
    outgoing = place_shares(
        enc_share.reshape(span_count, rows, depth), picked, encodings.shape[0]
    )
    grad_encodings = lax.all_to_all(outgoing, "seq", split_axis=0, concat_axis=0, tiled=True)
    around = [k % chips for k in range(1, chips + 1)]
    branch = ring_reduce(branch_term, pairs, around)
    grad_hidden = ring_reduce(hidden_term, pairs, around)
    return (branch, grad_hidden, grad_encodings)


def solution(mesh):
    return jax.shard_map(
        on_device,
        mesh=mesh,
        in_specs=(
            P("seq", "mp"),
            P("seq", "mp", None),
            P(),
            P(None, "mp"),
            P(None, "mp"),
            P(None, "mp"),
            P("mp", None),
            P("seq", "mp"),
        ),
        out_specs=(P("seq", "mp"), P("seq", "mp"), P("seq", "mp", None)),
        check_vma=False,
    )
```

```python
import functools

import jax
import jax.numpy as jnp
from jax import lax
from jax.experimental import pallas as pl
from jax.experimental.pallas import tpu as pltpu
from jax.sharding import PartitionSpec as P

DH = 128
SPAN = 64
LEAD = SPAN - 1
CORES = 2
F32 = jnp.float32
BF16 = jnp.bfloat16
NT = (((1,), (1,)), ((), ()))
NN = (((1,), (0,)), ((), ()))
TN = (((0,), (0,)), ((), ()))


def ring_pairs(count):
    chips = count // CORES
    up = [(CORES * i, CORES * ((i + 1) % chips)) for i in range(chips)]
    down = [(CORES * i + 1, CORES * ((i - 1) % chips) + 1) for i in range(chips)]
    return up + down


def swap_cores(value):
    count = lax.axis_size("mp")
    return lax.ppermute(value, "mp", [(i, i ^ 1) for i in range(count)])


def ring_steps(block, pairs, steps):
    blocks = []
    for _ in range(steps):
        block = lax.ppermute(block, "mp", pairs)
        blocks.append(block)
    return blocks


def ring_reduce(term, pairs, places, total=None):
    for place in places:
        own = term(place)
        if total is not None:
            own = own + lax.ppermute(total, "mp", pairs).astype(F32)
        total = own.astype(BF16)
    return total


def one_way(count, step):
    return [(i, (i + CORES * step) % count) for i in range(count)]


def both_ways_gather(block, up, down, chips):
    steps = chips // 2 - 1
    half = block.shape[0] // 2
    behind, ahead = ring_steps(block, up, steps), ring_steps(block, down, steps)
    opposite = jnp.concatenate(
        [
            lax.ppermute(behind[-1][:half], "mp", up),
            lax.ppermute(ahead[-1][half:], "mp", down),
        ],
        axis=0,
    )
    return [block, *behind, *ahead, opposite]


def both_ways_reduce(term, opposite, up, down, chips):
    steps = chips // 2 - 1
    half = opposite[0].shape[0]
    got_up = lax.ppermute(opposite[0], "mp", up).astype(F32)
    got_down = lax.ppermute(opposite[1], "mp", down).astype(F32)
    to_up, to_down = term(chips - 2), term(steps)
    to_up = jnp.concatenate([to_up[:half] + got_up, to_up[half:]], axis=0)
    to_down = jnp.concatenate([to_down[:half], to_down[half:] + got_down], axis=0)
    for left in range(steps - 1, -1, -1):
        got_up = lax.ppermute(to_up.astype(BF16), "mp", up).astype(F32)
        got_down = lax.ppermute(to_down.astype(BF16), "mp", down).astype(F32)
        if left:
            to_up, to_down = term(steps + left) + got_up, term(left) + got_down
    return (term(0) + got_up + got_down).astype(BF16)


def after(value, *earlier):
    return lax.optimization_barrier((value, *earlier))[0]


def ring_weights_kernel(places, wq_own, wq_sib, wo_own, wo_sib, wq_ring, wo_ring):
    columns = wq_own.shape[1]
    wq_ring[0, :, :columns] = wq_own[...]
    wq_ring[0, :, columns:] = wq_sib[...]
    wo_ring[0, :columns, :] = wo_own[...]
    wo_ring[0, columns:, :] = wo_sib[...]


def ring_weights(places, w_query, wq_sib, w_out, wo_sib, width):
    count = places.shape[0]
    columns = w_query.shape[1]
    by_rows = pl.BlockSpec((width, columns), lambda k, at: (at[k], 0))
    by_columns = pl.BlockSpec((columns, width), lambda k, at: (0, at[k]))
    return pl.pallas_call(
        ring_weights_kernel,
        grid_spec=pltpu.PrefetchScalarGridSpec(
            num_scalar_prefetch=1,
            grid=(count,),
            in_specs=[by_rows, by_rows, by_columns, by_columns],
            out_specs=[
                pl.BlockSpec((1, width, CORES * columns), lambda k, at: (k, 0, 0)),
                pl.BlockSpec((1, CORES * columns, width), lambda k, at: (k, 0, 0)),
            ],
        ),
        out_shape=[
            jax.ShapeDtypeStruct((count, width, CORES * columns), BF16),
            jax.ShapeDtypeStruct((count, CORES * columns, width), BF16),
        ],
    )(places, w_query, wq_sib, w_out, wo_sib)


def copy_kernel(given, out):
    out[...] = given[...]


def copy_of(given, steps=4):
    block = pl.BlockSpec((given.shape[0] // steps, *given.shape[1:]), lambda i: (i, 0, 0))
    return pl.pallas_call(
        copy_kernel,
        grid=(steps,),
        in_specs=[block],
        out_specs=block,
        out_shape=jax.ShapeDtypeStruct(given.shape, given.dtype),
    )(given)


def pick_kernel(picked, held, out):
    for u in range(out.shape[0]):
        out[u] = held[picked[u]]


def pick(held, picked):
    count = picked.shape[0]
    return pl.pallas_call(
        pick_kernel,
        grid_spec=pltpu.PrefetchScalarGridSpec(
            num_scalar_prefetch=1,
            grid=(1,),
            in_specs=[pl.BlockSpec(held.shape, lambda i, at: (0, 0, 0))],
            out_specs=pl.BlockSpec((count, *held.shape[1:]), lambda i, at: (0, 0, 0)),
        ),
        out_shape=jax.ShapeDtypeStruct((count, *held.shape[1:]), BF16),
    )(picked, held)


def place_kernel(picked, shares, out):
    out[...] = jnp.zeros_like(out)
    for u in range(shares.shape[0]):
        out[picked[u]] = shares[u]


def place_shares(shares, picked, slots):
    shape = (slots, *shares.shape[1:])
    return pl.pallas_call(
        place_kernel,
        grid_spec=pltpu.PrefetchScalarGridSpec(
            num_scalar_prefetch=1,
            grid=(1,),
            in_specs=[pl.BlockSpec(shares.shape, lambda i, at: (0, 0, 0))],
            out_specs=pl.BlockSpec(shape, lambda i, at: (0, 0, 0)),
        ),
        out_shape=jax.ShapeDtypeStruct(shape, BF16),
    )(picked, shares)


def project_part_kernel(dims, *refs):
    *blocks, weights, out = refs
    total = None
    for k, block in enumerate(blocks):
        part = lax.dot_general(block[...], weights[k], dims, preferred_element_type=F32)
        total = part if total is None else total + part
    out[...] = total.astype(BF16)


def project_part(blocks, weights, dims, tile=256):
    tokens, width = blocks[0].shape
    count, wide = len(blocks), CORES * width
    return pl.pallas_call(
        functools.partial(project_part_kernel, dims),
        grid=(tokens // tile,),
        in_specs=[pl.BlockSpec((tile, width), lambda i: (i, 0))] * count
        + [pl.BlockSpec((count, *weights.shape[1:]), lambda i: (0, 0, 0))],
        out_specs=pl.BlockSpec((tile, wide), lambda i: (i, 0)),
        out_shape=jax.ShapeDtypeStruct((tokens, wide), BF16),
        compiler_params=pltpu.CompilerParams(vmem_limit_bytes=32 * 1024 * 1024),
    )(*blocks, weights)


def project_rest_kernel(count, *refs):
    hidden, cot = refs[:count], refs[count : 2 * count]
    wq, wo, q_part, g_part, own, sib = refs[2 * count :]
    columns = own.shape[1] // 2
    for at, (blocks, weights, part, dims) in enumerate(
        ((hidden, wq, q_part, NN), (cot, wo, g_part, NT))
    ):
        total = part[...].astype(F32)
        for k, block in enumerate(blocks):
            total += lax.dot_general(block[...], weights[k], dims, preferred_element_type=F32)
        col = slice(at * columns, (at + 1) * columns)
        own[:, col] = total[:, :columns].astype(BF16)
        sib[:, col] = total[:, columns:].astype(BF16)


def project_rest(hidden, cot, wq, wo, q_part, g_part, tokens, tile):
    width = hidden[0].shape[1]
    count, wide = len(hidden), CORES * width
    rows = pl.BlockSpec((tile, width), lambda i: (i, 0))
    wide_rows = pl.BlockSpec((tile, wide), lambda i: (i, 0))
    last = wq.shape[0] // count - 1
    return pl.pallas_call(
        functools.partial(project_rest_kernel, count),
        grid=(tokens // tile,),
        in_specs=[rows] * (2 * count)
        + [
            pl.BlockSpec((count, *wq.shape[1:]), lambda i: (last, 0, 0)),
            pl.BlockSpec((count, *wo.shape[1:]), lambda i: (last, 0, 0)),
            wide_rows,
            wide_rows,
        ],
        out_specs=[wide_rows, wide_rows],
        out_shape=[
            jax.ShapeDtypeStruct((tokens, wide), BF16),
            jax.ShapeDtypeStruct((tokens, wide), BF16),
        ],
        compiler_params=pltpu.CompilerParams(vmem_limit_bytes=48 * 1024 * 1024),
    )(*hidden, *cot, wq, wo, q_part, g_part)


def key_values_kernel(*refs):
    *blocks, weights, own, sib = refs
    width = own.shape[2]
    for k, block in enumerate(blocks):
        total = jnp.dot(block[...], weights[...], preferred_element_type=F32).astype(BF16)
        own[k] = total[:, :width]
        sib[k] = total[:, width:]


def key_values(blocks, weights):
    rows, depth = blocks[0].shape
    count, width = len(blocks), weights.shape[1] // CORES
    out = jax.ShapeDtypeStruct((count, rows, width), BF16)
    return pl.pallas_call(
        key_values_kernel,
        out_shape=[out, out],
        compiler_params=pltpu.CompilerParams(vmem_limit_bytes=32 * 1024 * 1024),
    )(*blocks, weights)


def attention_kernel(part_count, own, got, own_next, got_next, before, *refs):
    kv_parts, refs = refs[:part_count], refs[part_count:]
    out, out_after, gkv_own, gkv_sib, carry = refs[-5:]
    chips, spans, rows, width = gkv_own.shape
    columns = width // 2
    heads = columns // DH
    half = chips * rows
    scale = DH ** (-0.5)
    tokens = own.shape[0]

    here = own[...].astype(F32) + got[...].astype(F32)
    following = own_next[...].astype(F32) + got_next[...].astype(F32)
    asked = jnp.concatenate([here[LEAD:], following[:LEAD]], axis=0).astype(BF16)

    todo = []
    for u in range(spans):
        tok = slice(u * SPAN, (u + 1) * SPAN)
        key_values = jnp.concatenate(
            [part[:, u, :, :].reshape(part.shape[0] * rows, width) for part in kv_parts],
            axis=0,
        )
        for h in range(heads):
            col = slice(h * DH, (h + 1) * DH)
            vcol = slice(columns + h * DH, columns + (h + 1) * DH)
            todo.append((u, col, vcol, asked[tok, col], asked[tok, vcol], key_values[:, col], key_values[:, vcol]))
    scores = [lax.dot_general(q, k, NT, preferred_element_type=F32) * scale for _, _, _, q, _, k, _ in todo]
    grad_w = [lax.dot_general(g, v, NT, preferred_element_type=F32) for _, _, _, _, g, _, v in todo]
    raised = [jnp.exp(x - jnp.max(x, axis=-1, keepdims=True)) for x in scores]
    weights = [x * (1.0 / jnp.sum(x, axis=-1, keepdims=True)) for x in raised]
    low = [x.astype(BF16) for x in weights]
    inner = [jnp.sum(x * y, axis=-1, keepdims=True) for x, y in zip(weights, grad_w)]
    grad_s = [(x * (y - z) * scale).astype(BF16) for x, y, z in zip(weights, grad_w, inner)]
    attended = [jnp.dot(x, t[6], preferred_element_type=F32) for x, t in zip(low, todo)]
    grad_q = [jnp.dot(x, t[5], preferred_element_type=F32) for x, t in zip(grad_s, todo)]
    for (u, col, vcol, q, g, _, _), x, y in zip(todo, low, grad_s):
        gk = lax.dot_general(y, q, TN, preferred_element_type=F32).astype(BF16)
        gv = lax.dot_general(x, g, TN, preferred_element_type=F32).astype(BF16)
        gkv_own[:, u, :, col] = gk[:half].reshape(chips, rows, DH)
        gkv_sib[:, u, :, col] = gk[half:].reshape(chips, rows, DH)
        gkv_own[:, u, :, vcol] = gv[:half].reshape(chips, rows, DH)
        gkv_sib[:, u, :, vcol] = gv[half:].reshape(chips, rows, DH)
    by_span = [
        jnp.concatenate(attended[u * heads : (u + 1) * heads] + grad_q[u * heads : (u + 1) * heads], axis=1)
        for u in range(spans)
    ]
    answers = jnp.concatenate(by_span, axis=0)
    earlier = jnp.where(pl.program_id(0) == 0, before[...].astype(F32), carry[...])
    out[...] = jnp.concatenate([earlier[:LEAD], answers[: tokens - LEAD]], axis=0).astype(BF16)
    left = jnp.concatenate([answers[tokens - LEAD:], jnp.zeros((1, answers.shape[1]), F32)], axis=0)
    carry[...] = left
    out_after[...] = left.astype(BF16)


def attention(own, got, own_next, got_next, before, kv_parts, first, steps, results=(), per_step=4):
    _, spans, rows, width = kv_parts[0].shape
    chips = sum(part.shape[0] for part in kv_parts) // CORES
    tokens, wide = own.shape
    following = first + 1 if own_next is own else 0
    tok = pl.BlockSpec((per_step * SPAN, wide), lambda i: (first + i, 0))
    nexts = pl.BlockSpec((SPAN, wide), lambda i: ((following + i) * per_step, 0))
    whole = pl.BlockSpec((SPAN, wide), lambda i: (0, 0))

    def kvs(count):
        return pl.BlockSpec((count, per_step, rows, width), lambda i: (0, first + i, 0, 0))

    kv_type = jax.ShapeDtypeStruct((chips, spans, rows, width), BF16)
    given = 5 + len(kv_parts)
    return pl.pallas_call(
        functools.partial(attention_kernel, len(kv_parts)),
        grid=(steps,),
        in_specs=[tok, tok, nexts, nexts, whole]
        + [kvs(part.shape[0]) for part in kv_parts]
        + [pl.BlockSpec(memory_space=pl.ANY)] * len(results),
        out_specs=[tok, whole, kvs(chips), kvs(chips)],
        out_shape=[
            jax.ShapeDtypeStruct((tokens, wide), BF16),
            jax.ShapeDtypeStruct((SPAN, wide), BF16),
            kv_type,
            kv_type,
        ],
        scratch_shapes=[pltpu.VMEM((SPAN, wide), F32)],
        input_output_aliases=dict(zip(range(given, given + len(results)), (0, 2, 3))),
        compiler_params=pltpu.CompilerParams(vmem_limit_bytes=48 * 1024 * 1024),
    )(own, got, own_next, got_next, before, *kv_parts, *results)


def on_device(hidden, encodings, span_owner, w_query, w_key, w_value, w_out, cotangent):
    seq_count = lax.axis_size("seq")
    shard_index = lax.axis_index("seq")
    mp_count = lax.axis_size("mp")
    chips = mp_count // CORES
    place = lax.axis_index("mp")
    core = place % CORES
    chip = place // CORES
    pairs = ring_pairs(mp_count)
    heading = 1 - 2 * core
    origin = [(chip - heading * k + chips) % chips for k in range(chips)]

    capacity = encodings.shape[0] // seq_count
    token_count, width = hidden.shape
    span_count = token_count // SPAN
    rows, depth = encodings.shape[1:]
    columns = w_query.shape[1]

    owners = lax.dynamic_slice_in_dim(span_owner[:, 0], shard_index * span_count, span_count)
    positions = jnp.arange(span_count, dtype=jnp.int32)
    earlier = (owners[:, None] == owners[None, :]) & (positions[None, :] < positions[:, None])
    picked = owners * capacity + jnp.sum(earlier.astype(jnp.int32), axis=1)

    def to_shard(value, steps, across):
        shards = range(max(0, -steps), min(seq_count, seq_count - steps))
        moves = [
            (d * mp_count + i, (d + steps) * mp_count + (i ^ across))
            for d in shards
            for i in range(mp_count)
        ]
        return lax.ppermute(value, ("seq", "mp"), moves)

    up, down = one_way(mp_count, 1), one_way(mp_count, -1)

    wk_sib, wv_sib = swap_cores(w_key), swap_cores(w_value)
    wkv_full = jnp.concatenate([w_key, w_value, wk_sib, wv_sib], axis=1)
    places = jnp.stack([CORES * source + core for source in origin])
    wq_ring, wo_ring = ring_weights(
        places, w_query, swap_cores(w_query), w_out, swap_cores(w_out), width
    )

    received = lax.all_to_all(
        after(encodings, wk_sib), "seq", split_axis=0, concat_axis=0, tiled=True
    )
    shard_part = pick(received, picked).reshape(span_count * rows, depth)
    early = chips // 2
    hidden_blocks = [hidden] + ring_steps(hidden, pairs, early)
    cot_blocks = [cotangent] + ring_steps(cotangent, pairs, early)
    hidden_last, cot_last, wq_ring, wo_ring = lax.optimization_barrier(
        (hidden_blocks.pop(), cot_blocks.pop(), wq_ring, wo_ring)
    )
    hidden_late = [hidden_last] + ring_steps(hidden_last, pairs, chips - early - 2)
    cot_late = [cot_last] + ring_steps(cot_last, pairs, chips - early - 2)
    enc_blocks = both_ways_gather(shard_part, up, down, chips)

    q_part = project_part(hidden_blocks, wq_ring, NN)
    g_part = project_part(cot_blocks, wo_ring, NT)
    kv_own_a, kv_send_a = key_values([enc_blocks[k] for k in (0, 1, 2, 4, 5)], wkv_full)
    hidden_last, cot_last, q_part, g_part, kv_own_a, kv_send_a = lax.optimization_barrier(
        (hidden_late[-1], cot_late[-1], q_part, g_part, kv_own_a, kv_send_a)
    )
    hidden_late[-1], cot_late[-1] = hidden_last, cot_last
    hidden_late += ring_steps(hidden_last, pairs, 1)
    cot_late += ring_steps(cot_last, pairs, 1)
    kv_sib_a = swap_cores(kv_send_a)
    kv_own_b, kv_send_b = key_values([enc_blocks[3], enc_blocks[6], enc_blocks[7]], wkv_full)
    kv_sib_b = swap_cores(kv_send_b)
    q_part, g_part, _ = lax.optimization_barrier((q_part, g_part, kv_send_b))
    own, send = project_rest(
        hidden_late, cot_late, wq_ring, wo_ring, q_part, g_part, token_count, 256
    )
    got = swap_cores(send)
    own_after, got_after = to_shard(own[:SPAN], -1, 0), to_shard(send[:SPAN], -1, 1)
    order = [0, 1, 2, 4, 5, 3, 6, 7]
    kv_parts = [
        part.reshape(-1, span_count, rows, 2 * columns)
        for part in (kv_own_a, kv_own_b, kv_sib_a, kv_sib_b)
    ]
    steps = span_count // 4
    nothing = jnp.zeros((SPAN, 2 * columns), BF16)
    answers, answers_after, gkv_own, gkv_sib = attention(
        own, got, own, got, nothing, kv_parts, 0, steps - 1
    )
    answers, answers_after, gkv_own, gkv_sib = attention(
        own,
        got,
        own_after,
        got_after,
        answers_after,
        kv_parts,
        steps - 1,
        1,
        (answers, gkv_own, gkv_sib),
    )
    gkv_full = jnp.concatenate([gkv_own, swap_cores(gkv_sib)], axis=3).reshape(
        chips, span_count * rows, 4 * columns
    )
    answers_got = swap_cores(answers)
    lead_own, lead_got = to_shard(answers_after, 1, 0), to_shard(answers_after, 1, 1)
    answers = answers.at[:SPAN].add(lead_own)
    answers_got = answers_got.at[:SPAN].add(lead_got)
    att_full = jnp.concatenate([answers[:, :columns], answers_got[:, :columns]], axis=1)
    gq_full = jnp.concatenate([answers[:, columns:], answers_got[:, columns:]], axis=1)

    def enc_term(k):
        return lax.dot_general(
            gkv_full[order.index(k)], wkv_full, NT, preferred_element_type=F32
        )

    def branch_term(k):
        return jnp.dot(att_full, wo_ring[k], preferred_element_type=F32)

    def hidden_term(k):
        return lax.dot_general(gq_full, wq_ring[k], NT, preferred_element_type=F32)

    opposite = enc_term(chips - 1).astype(BF16)
    half = opposite.shape[0] // 2
    opposite = (opposite[:half], opposite[half:])
    att_full, gq_full, opposite = lax.optimization_barrier((att_full, gq_full, opposite))
    enc_share = both_ways_reduce(enc_term, opposite, up, down, chips)
    outgoing = place_shares(
        enc_share.reshape(span_count, rows, depth), picked, encodings.shape[0]
    )
    grad_encodings = lax.all_to_all(outgoing, "seq", split_axis=0, concat_axis=0, tiled=True)
    grad_encodings = copy_of(grad_encodings)
    around = [k % chips for k in range(1, chips + 1)]
    branch = ring_reduce(branch_term, pairs, around)
    grad_hidden = ring_reduce(hidden_term, pairs, around)
    return (branch, grad_hidden, grad_encodings)


def solution(mesh):
    return jax.shard_map(
        on_device,
        mesh=mesh,
        in_specs=(
            P("seq", "mp"),
            P("seq", "mp", None),
            P(),
            P(None, "mp"),
            P(None, "mp"),
            P(None, "mp"),
            P("mp", None),
            P("seq", "mp"),
        ),
        out_specs=(P("seq", "mp"), P("seq", "mp"), P("seq", "mp", None)),
        check_vma=False,
    )
```

```python
import functools

import jax
import jax.numpy as jnp
from jax import lax
from jax.experimental import pallas as pl
from jax.experimental.pallas import tpu as pltpu
from jax.sharding import PartitionSpec as P

DH = 128
SPAN = 64
LEAD = SPAN - 1
CORES = 2
F32 = jnp.float32
BF16 = jnp.bfloat16
NT = (((1,), (1,)), ((), ()))
NN = (((1,), (0,)), ((), ()))
TN = (((0,), (0,)), ((), ()))


def ring_pairs(count):
    chips = count // CORES
    up = [(CORES * i, CORES * ((i + 1) % chips)) for i in range(chips)]
    down = [(CORES * i + 1, CORES * ((i - 1) % chips) + 1) for i in range(chips)]
    return up + down


def swap_cores(value):
    count = lax.axis_size("mp")
    return lax.ppermute(value, "mp", [(i, i ^ 1) for i in range(count)])


def ring_steps(block, pairs, steps):
    blocks = []
    for _ in range(steps):
        block = lax.ppermute(block, "mp", pairs)
        blocks.append(block)
    return blocks


def ring_reduce(term, pairs, places, total=None):
    for place in places:
        own = term(place)
        if total is not None:
            own = own + lax.ppermute(total, "mp", pairs).astype(F32)
        total = own.astype(BF16)
    return total


def one_way(count, step):
    return [(i, (i + CORES * step) % count) for i in range(count)]


def both_ways_gather(block, up, down, chips):
    steps = chips // 2 - 1
    half = block.shape[0] // 2
    behind, ahead = ring_steps(block, up, steps), ring_steps(block, down, steps)
    opposite = jnp.concatenate(
        [
            lax.ppermute(behind[-1][:half], "mp", up),
            lax.ppermute(ahead[-1][half:], "mp", down),
        ],
        axis=0,
    )
    return [block, *behind, *ahead, opposite]


def both_ways_reduce(term, opposite, up, down, chips):
    steps = chips // 2 - 1
    half = opposite[0].shape[0]
    got_up = lax.ppermute(opposite[0], "mp", up).astype(F32)
    got_down = lax.ppermute(opposite[1], "mp", down).astype(F32)
    to_up, to_down = term(chips - 2), term(steps)
    to_up = jnp.concatenate([to_up[:half] + got_up, to_up[half:]], axis=0)
    to_down = jnp.concatenate([to_down[:half], to_down[half:] + got_down], axis=0)
    for left in range(steps - 1, -1, -1):
        got_up = lax.ppermute(to_up.astype(BF16), "mp", up).astype(F32)
        got_down = lax.ppermute(to_down.astype(BF16), "mp", down).astype(F32)
        if left:
            to_up, to_down = term(steps + left) + got_up, term(left) + got_down
    return (term(0) + got_up + got_down).astype(BF16)


def after(value, *earlier):
    return lax.optimization_barrier((value, *earlier))[0]


def ring_weights_kernel(places, wq_own, wq_sib, wo_own, wo_sib, wq_ring, wo_ring):
    columns = wq_own.shape[1]
    wq_ring[0, :, :columns] = wq_own[...]
    wq_ring[0, :, columns:] = wq_sib[...]
    wo_ring[0, :columns, :] = wo_own[...]
    wo_ring[0, columns:, :] = wo_sib[...]


def ring_weights(places, w_query, wq_sib, w_out, wo_sib, width):
    count = places.shape[0]
    columns = w_query.shape[1]
    by_rows = pl.BlockSpec((width, columns), lambda k, at: (at[k], 0))
    by_columns = pl.BlockSpec((columns, width), lambda k, at: (0, at[k]))
    return pl.pallas_call(
        ring_weights_kernel,
        grid_spec=pltpu.PrefetchScalarGridSpec(
            num_scalar_prefetch=1,
            grid=(count,),
            in_specs=[by_rows, by_rows, by_columns, by_columns],
            out_specs=[
                pl.BlockSpec((1, width, CORES * columns), lambda k, at: (k, 0, 0)),
                pl.BlockSpec((1, CORES * columns, width), lambda k, at: (k, 0, 0)),
            ],
        ),
        out_shape=[
            jax.ShapeDtypeStruct((count, width, CORES * columns), BF16),
            jax.ShapeDtypeStruct((count, CORES * columns, width), BF16),
        ],
    )(places, w_query, wq_sib, w_out, wo_sib)


def copy_kernel(given, out):
    out[...] = given[...]


def copy_of(given, steps=4):
    block = pl.BlockSpec((given.shape[0] // steps, *given.shape[1:]), lambda i: (i, 0, 0))
    return pl.pallas_call(
        copy_kernel,
        grid=(steps,),
        in_specs=[block],
        out_specs=block,
        out_shape=jax.ShapeDtypeStruct(given.shape, given.dtype),
    )(given)


def pick_kernel(picked, held, out):
    for u in range(out.shape[0]):
        out[u] = held[picked[u]]


def pick(held, picked):
    count = picked.shape[0]
    return pl.pallas_call(
        pick_kernel,
        grid_spec=pltpu.PrefetchScalarGridSpec(
            num_scalar_prefetch=1,
            grid=(1,),
            in_specs=[pl.BlockSpec(held.shape, lambda i, at: (0, 0, 0))],
            out_specs=pl.BlockSpec((count, *held.shape[1:]), lambda i, at: (0, 0, 0)),
        ),
        out_shape=jax.ShapeDtypeStruct((count, *held.shape[1:]), BF16),
    )(picked, held)


def place_kernel(picked, shares, out):
    out[...] = jnp.zeros_like(out)
    for u in range(shares.shape[0]):
        out[picked[u]] = shares[u]


def place_shares(shares, picked, slots):
    shape = (slots, *shares.shape[1:])
    return pl.pallas_call(
        place_kernel,
        grid_spec=pltpu.PrefetchScalarGridSpec(
            num_scalar_prefetch=1,
            grid=(1,),
            in_specs=[pl.BlockSpec(shares.shape, lambda i, at: (0, 0, 0))],
            out_specs=pl.BlockSpec(shape, lambda i, at: (0, 0, 0)),
        ),
        out_shape=jax.ShapeDtypeStruct(shape, BF16),
    )(picked, shares)


def project_part_kernel(dims, *refs):
    *blocks, weights, out = refs
    total = None
    for k, block in enumerate(blocks):
        part = lax.dot_general(block[...], weights[k], dims, preferred_element_type=F32)
        total = part if total is None else total + part
    out[...] = total.astype(BF16)


def project_part(blocks, weights, dims, tile=256):
    tokens, width = blocks[0].shape
    count, wide = len(blocks), CORES * width
    return pl.pallas_call(
        functools.partial(project_part_kernel, dims),
        grid=(tokens // tile,),
        in_specs=[pl.BlockSpec((tile, width), lambda i: (i, 0))] * count
        + [pl.BlockSpec((count, *weights.shape[1:]), lambda i: (0, 0, 0))],
        out_specs=pl.BlockSpec((tile, wide), lambda i: (i, 0)),
        out_shape=jax.ShapeDtypeStruct((tokens, wide), BF16),
        compiler_params=pltpu.CompilerParams(vmem_limit_bytes=32 * 1024 * 1024),
    )(*blocks, weights)


def project_rest_kernel(count, *refs):
    hidden, cot = refs[:count], refs[count : 2 * count]
    wq, wo, q_part, g_part, own, sib = refs[2 * count :]
    columns = own.shape[1] // 2
    for at, (blocks, weights, part, dims) in enumerate(
        ((hidden, wq, q_part, NN), (cot, wo, g_part, NT))
    ):
        total = part[...].astype(F32)
        for k, block in enumerate(blocks):
            total += lax.dot_general(block[...], weights[k], dims, preferred_element_type=F32)
        col = slice(at * columns, (at + 1) * columns)
        own[:, col] = total[:, :columns].astype(BF16)
        sib[:, col] = total[:, columns:].astype(BF16)


def project_rest(hidden, cot, wq, wo, q_part, g_part, tokens, tile):
    width = hidden[0].shape[1]
    count, wide = len(hidden), CORES * width
    rows = pl.BlockSpec((tile, width), lambda i: (i, 0))
    wide_rows = pl.BlockSpec((tile, wide), lambda i: (i, 0))
    last = wq.shape[0] // count - 1
    return pl.pallas_call(
        functools.partial(project_rest_kernel, count),
        grid=(tokens // tile,),
        in_specs=[rows] * (2 * count)
        + [
            pl.BlockSpec((count, *wq.shape[1:]), lambda i: (last, 0, 0)),
            pl.BlockSpec((count, *wo.shape[1:]), lambda i: (last, 0, 0)),
            wide_rows,
            wide_rows,
        ],
        out_specs=[wide_rows, wide_rows],
        out_shape=[
            jax.ShapeDtypeStruct((tokens, wide), BF16),
            jax.ShapeDtypeStruct((tokens, wide), BF16),
        ],
        compiler_params=pltpu.CompilerParams(vmem_limit_bytes=48 * 1024 * 1024),
    )(*hidden, *cot, wq, wo, q_part, g_part)


def key_values_kernel(*refs):
    *blocks, weights, own, sib = refs
    width = own.shape[2]
    for k, block in enumerate(blocks):
        total = jnp.dot(block[...], weights[...], preferred_element_type=F32).astype(BF16)
        own[k] = total[:, :width]
        sib[k] = total[:, width:]


def key_values(blocks, weights):
    rows, depth = blocks[0].shape
    count, width = len(blocks), weights.shape[1] // CORES
    out = jax.ShapeDtypeStruct((count, rows, width), BF16)
    return pl.pallas_call(
        key_values_kernel,
        out_shape=[out, out],
        compiler_params=pltpu.CompilerParams(vmem_limit_bytes=32 * 1024 * 1024),
    )(*blocks, weights)


def attention_kernel(part_count, own, got, own_next, got_next, before, *refs):
    kv_parts, refs = refs[:part_count], refs[part_count:]
    out, out_after, gkv_own, gkv_sib, carry = refs[-5:]
    chips, spans, rows, width = gkv_own.shape
    columns = width // 2
    heads = columns // DH
    half = chips * rows
    scale = DH ** (-0.5)
    tokens = own.shape[0]

    here = own[...].astype(F32) + got[...].astype(F32)
    following = own_next[...].astype(F32) + got_next[...].astype(F32)
    asked = jnp.concatenate([here[LEAD:], following[:LEAD]], axis=0).astype(BF16)

    todo = []
    for u in range(spans):
        tok = slice(u * SPAN, (u + 1) * SPAN)
        key_values = jnp.concatenate(
            [part[:, u, :, :].reshape(part.shape[0] * rows, width) for part in kv_parts],
            axis=0,
        )
        for h in range(heads):
            col = slice(h * DH, (h + 1) * DH)
            vcol = slice(columns + h * DH, columns + (h + 1) * DH)
            todo.append((u, col, vcol, asked[tok, col], asked[tok, vcol], key_values[:, col], key_values[:, vcol]))
    scores = [lax.dot_general(q, k, NT, preferred_element_type=F32) * scale for _, _, _, q, _, k, _ in todo]
    grad_w = [lax.dot_general(g, v, NT, preferred_element_type=F32) for _, _, _, _, g, _, v in todo]
    raised = [jnp.exp(x - jnp.max(x, axis=-1, keepdims=True)) for x in scores]
    weights = [x * (1.0 / jnp.sum(x, axis=-1, keepdims=True)) for x in raised]
    low = [x.astype(BF16) for x in weights]
    inner = [jnp.sum(x * y, axis=-1, keepdims=True) for x, y in zip(weights, grad_w)]
    grad_s = [(x * (y - z) * scale).astype(BF16) for x, y, z in zip(weights, grad_w, inner)]
    attended = [jnp.dot(x, t[6], preferred_element_type=F32) for x, t in zip(low, todo)]
    grad_q = [jnp.dot(x, t[5], preferred_element_type=F32) for x, t in zip(grad_s, todo)]
    for (u, col, vcol, q, g, _, _), x, y in zip(todo, low, grad_s):
        gk = lax.dot_general(y, q, TN, preferred_element_type=F32).astype(BF16)
        gv = lax.dot_general(x, g, TN, preferred_element_type=F32).astype(BF16)
        gkv_own[:, u, :, col] = gk[:half].reshape(chips, rows, DH)
        gkv_sib[:, u, :, col] = gk[half:].reshape(chips, rows, DH)
        gkv_own[:, u, :, vcol] = gv[:half].reshape(chips, rows, DH)
        gkv_sib[:, u, :, vcol] = gv[half:].reshape(chips, rows, DH)
    by_span = [
        jnp.concatenate(attended[u * heads : (u + 1) * heads] + grad_q[u * heads : (u + 1) * heads], axis=1)
        for u in range(spans)
    ]
    answers = jnp.concatenate(by_span, axis=0)
    earlier = jnp.where(pl.program_id(0) == 0, before[...].astype(F32), carry[...])
    out[...] = jnp.concatenate([earlier[:LEAD], answers[: tokens - LEAD]], axis=0).astype(BF16)
    left = jnp.concatenate([answers[tokens - LEAD:], jnp.zeros((1, answers.shape[1]), F32)], axis=0)
    carry[...] = left
    out_after[...] = left.astype(BF16)


def attention(own, got, own_next, got_next, before, kv_parts, first, steps, results=(), per_step=4):
    _, spans, rows, width = kv_parts[0].shape
    chips = sum(part.shape[0] for part in kv_parts) // CORES
    tokens, wide = own.shape
    following = first + 1 if own_next is own else 0
    tok = pl.BlockSpec((per_step * SPAN, wide), lambda i: (first + i, 0))
    nexts = pl.BlockSpec((SPAN, wide), lambda i: ((following + i) * per_step, 0))
    whole = pl.BlockSpec((SPAN, wide), lambda i: (0, 0))

    def kvs(count):
        return pl.BlockSpec((count, per_step, rows, width), lambda i: (0, first + i, 0, 0))

    kv_type = jax.ShapeDtypeStruct((chips, spans, rows, width), BF16)
    given = 5 + len(kv_parts)
    return pl.pallas_call(
        functools.partial(attention_kernel, len(kv_parts)),
        grid=(steps,),
        in_specs=[tok, tok, nexts, nexts, whole]
        + [kvs(part.shape[0]) for part in kv_parts]
        + [pl.BlockSpec(memory_space=pl.ANY)] * len(results),
        out_specs=[tok, whole, kvs(chips), kvs(chips)],
        out_shape=[
            jax.ShapeDtypeStruct((tokens, wide), BF16),
            jax.ShapeDtypeStruct((SPAN, wide), BF16),
            kv_type,
            kv_type,
        ],
        scratch_shapes=[pltpu.VMEM((SPAN, wide), F32)],
        input_output_aliases=dict(zip(range(given, given + len(results)), (0, 2, 3))),
        compiler_params=pltpu.CompilerParams(vmem_limit_bytes=48 * 1024 * 1024),
    )(own, got, own_next, got_next, before, *kv_parts, *results)


def on_device(hidden, encodings, span_owner, w_query, w_key, w_value, w_out, cotangent):
    seq_count = lax.axis_size("seq")
    shard_index = lax.axis_index("seq")
    mp_count = lax.axis_size("mp")
    chips = mp_count // CORES
    place = lax.axis_index("mp")
    core = place % CORES
    chip = place // CORES
    pairs = ring_pairs(mp_count)
    heading = 1 - 2 * core
    origin = [(chip - heading * k + chips) % chips for k in range(chips)]

    capacity = encodings.shape[0] // seq_count
    token_count, width = hidden.shape
    span_count = token_count // SPAN
    rows, depth = encodings.shape[1:]
    columns = w_query.shape[1]

    owners = lax.dynamic_slice_in_dim(span_owner[:, 0], shard_index * span_count, span_count)
    positions = jnp.arange(span_count, dtype=jnp.int32)
    earlier = (owners[:, None] == owners[None, :]) & (positions[None, :] < positions[:, None])
    picked = owners * capacity + jnp.sum(earlier.astype(jnp.int32), axis=1)

    def to_shard(value, steps, across):
        shards = range(max(0, -steps), min(seq_count, seq_count - steps))
        moves = [
            (d * mp_count + i, (d + steps) * mp_count + (i ^ across))
            for d in shards
            for i in range(mp_count)
        ]
        return lax.ppermute(value, ("seq", "mp"), moves)

    up, down = one_way(mp_count, 1), one_way(mp_count, -1)

    wk_sib, wv_sib = swap_cores(w_key), swap_cores(w_value)
    wkv_full = jnp.concatenate([w_key, w_value, wk_sib, wv_sib], axis=1)
    places = jnp.stack([CORES * source + core for source in origin])
    wq_ring, wo_ring = ring_weights(
        places, w_query, swap_cores(w_query), w_out, swap_cores(w_out), width
    )

    received = lax.all_to_all(
        after(encodings, wk_sib), "seq", split_axis=0, concat_axis=0, tiled=True
    )
    shard_part = pick(received, picked).reshape(span_count * rows, depth)
    early = chips // 2
    hidden_blocks = [hidden] + ring_steps(hidden, pairs, early)
    cot_blocks = [cotangent] + ring_steps(cotangent, pairs, early)
    hidden_last, cot_last = hidden_blocks.pop(), cot_blocks.pop()
    hidden_late = [hidden_last] + ring_steps(hidden_last, pairs, 1)
    cot_late = [cot_last] + ring_steps(cot_last, pairs, 1)
    hidden_last, cot_last, wq_ring, wo_ring = lax.optimization_barrier(
        (hidden_late[-1], cot_late[-1], wq_ring, wo_ring)
    )
    hidden_late += ring_steps(hidden_last, pairs, chips - early - 3)
    cot_late += ring_steps(cot_last, pairs, chips - early - 3)
    enc_blocks = both_ways_gather(shard_part, up, down, chips)

    q_part = project_part(hidden_blocks, wq_ring, NN)
    g_part = project_part(cot_blocks, wo_ring, NT)
    kv_own_a, kv_send_a = key_values([enc_blocks[k] for k in (0, 1, 2, 4, 5)], wkv_full)
    hidden_last, cot_last, q_part, g_part = lax.optimization_barrier(
        (hidden_late[-1], cot_late[-1], q_part, g_part)
    )
    hidden_late[-1], cot_late[-1] = hidden_last, cot_last
    hidden_late += ring_steps(hidden_last, pairs, 1)
    cot_late += ring_steps(cot_last, pairs, 1)
    kv_sib_a = swap_cores(kv_send_a)
    kv_own_b, kv_send_b = key_values([enc_blocks[3], enc_blocks[6], enc_blocks[7]], wkv_full)
    kv_sib_b = swap_cores(kv_send_b)
    q_part, g_part, _ = lax.optimization_barrier((q_part, g_part, kv_send_b))
    own, send = project_rest(
        hidden_late, cot_late, wq_ring, wo_ring, q_part, g_part, token_count, 256
    )
    got = swap_cores(send)
    own_after, got_after = to_shard(own[:SPAN], -1, 0), to_shard(send[:SPAN], -1, 1)
    order = [0, 1, 2, 4, 5, 3, 6, 7]
    kv_parts = [
        part.reshape(-1, span_count, rows, 2 * columns)
        for part in (kv_own_a, kv_own_b, kv_sib_a, kv_sib_b)
    ]
    steps = span_count // 4
    nothing = jnp.zeros((SPAN, 2 * columns), BF16)
    answers, answers_after, gkv_own, gkv_sib = attention(
        own, got, own, got, nothing, kv_parts, 0, steps - 1
    )
    answers, answers_after, gkv_own, gkv_sib = attention(
        own,
        got,
        own_after,
        got_after,
        answers_after,
        kv_parts,
        steps - 1,
        1,
        (answers, gkv_own, gkv_sib),
    )
    gkv_full = jnp.concatenate([gkv_own, swap_cores(gkv_sib)], axis=3).reshape(
        chips, span_count * rows, 4 * columns
    )
    answers_got = swap_cores(answers)
    lead_own, lead_got = to_shard(answers_after, 1, 0), to_shard(answers_after, 1, 1)
    answers = answers.at[:SPAN].add(lead_own)
    answers_got = answers_got.at[:SPAN].add(lead_got)
    att_full = jnp.concatenate([answers[:, :columns], answers_got[:, :columns]], axis=1)
    gq_full = jnp.concatenate([answers[:, columns:], answers_got[:, columns:]], axis=1)

    def enc_term(k):
        return lax.dot_general(
            gkv_full[order.index(k)], wkv_full, NT, preferred_element_type=F32
        )

    def branch_term(k):
        return jnp.dot(att_full, wo_ring[k], preferred_element_type=F32)

    def hidden_term(k):
        return lax.dot_general(gq_full, wq_ring[k], NT, preferred_element_type=F32)

    opposite = enc_term(chips - 1).astype(BF16)
    half = opposite.shape[0] // 2
    opposite = (opposite[:half], opposite[half:])
    att_full, gq_full, opposite = lax.optimization_barrier((att_full, gq_full, opposite))
    enc_share = both_ways_reduce(enc_term, opposite, up, down, chips)
    outgoing = place_shares(
        enc_share.reshape(span_count, rows, depth), picked, encodings.shape[0]
    )
    grad_encodings = lax.all_to_all(outgoing, "seq", split_axis=0, concat_axis=0, tiled=True)
    grad_encodings = copy_of(grad_encodings)
    around = [k % chips for k in range(1, chips + 1)]
    branch = ring_reduce(branch_term, pairs, around)
    grad_hidden = ring_reduce(hidden_term, pairs, around)
    return (branch, grad_hidden, grad_encodings)


def solution(mesh):
    return jax.shard_map(
        on_device,
        mesh=mesh,
        in_specs=(
            P("seq", "mp"),
            P("seq", "mp", None),
            P(),
            P(None, "mp"),
            P(None, "mp"),
            P(None, "mp"),
            P("mp", None),
            P("seq", "mp"),
        ),
        out_specs=(P("seq", "mp"), P("seq", "mp"), P("seq", "mp", None)),
        check_vma=False,
    )
```
